32 devices in a mesh: expert: 4 (over y, x), blk: 8 (over z, core).
Axes of the slice: x: 2, y: 2, z: 4, core: 2. Of those that a mesh axis runs over, the one named last changes fastest.
Arguments:
- tokens: bfloat16 [512, 3072], P('expert', 'blk'), may hold values from -6 to 6
- routes: int32 [512, 2], P('expert'), may hold values from 0 to 3, all different within a row; in each aligned block of 128 rows (0 to 127, 128 to 255, ...) at most 128 rows name the same one
- labels: int32 [512], P('expert'), may hold values from 0 to 15
- gate_weight: bfloat16 [4, 3072, 8192], P('expert', None, 'blk'), may hold values from -0.109375 to 0.109375
- up_weight: bfloat16 [4, 3072, 8192], P('expert', None, 'blk'), may hold values from -0.109375 to 0.109375
Outputs:
- moment: bfloat16 [4, 8192, 8192], P('expert', 'blk')
- cross_moment: float32 [4, 8192, 16], P('expert', 'blk')
The draws below stay inside these ranges and needn't reach their ends.
Inputs may be any that keep to these rules, and one draw needn't show every extreme that they name: `routes`: in the rows of one token shard (128 rows), no expert is named by more than 128 rows, and in some shard one expert is named by exactly 128 rows; every expert is named by some row; a row names 2 different experts.
All inputs are finite; a program needn't handle non-finite values.
Results may differ from the reference program's by a relative error of at most 0.0057.
Values may be sent and summed in bfloat16 or wider, within the bound.
A program may use at most 128 MiB of HBM per device.

```python
import math
import jax
import jax.numpy as jnp
import numpy as np
from jax import lax

D = 3072
FF = 8192
TOP = 2
CLASSES = 16
TOK_E = 128
EXPERTS = 4
TOKENS = 512
SLOT = 128
CAP = 512
N_EXPERT = 4


def touch_ends(drawn, rng, low, high):
    longest = drawn.shape.index(max(drawn.shape))
    spots = []
    for shift in (0, 1):
        where = [jax.random.randint(jax.random.fold_in(rng, axis), (), 0, length) for axis, length in enumerate(drawn.shape)]
        where[longest] = (where[longest] + shift) % drawn.shape[longest]
        spots.append(tuple(where))
    return drawn.at[spots[0]].set(low).at[spots[1]].set(high)


def level_of(key, dims, split, smallest, high):
    def one(dim, shards_of):
        heights = jax.random.uniform(jax.random.fold_in(jax.random.fold_in(key, 6), dim), (shards_of,), jnp.float32, smallest / len(split), high / len(split))
        return jnp.repeat(jnp.exp(heights), dims[dim] // shards_of).reshape((-1,) + (1,) * (len(dims) - dim - 1))

    loudness = one(*split[0])
    for cut in split[1:]:
        loudness = loudness * one(*cut)
    return loudness


def deal_out(stream_key, own, number, rows, count, top, reach, skew):
    order = jax.random.permutation(stream_key, count)
    heavy_load, usual = shares(count, rows * top, reach, skew, True), shares(count, rows * top, reach, skew, False)
    places = jnp.arange(count)

    def named(lengths, rotation):
        used = int((lengths > 0).sum())
        fixed = max(1, used // 4)
        moved = fixed + (places - fixed + rotation * (used - fixed)) % max(1, count - fixed)
        return jnp.zeros((count,), jnp.int32).at[order[jnp.where(places < fixed, places, moved)]].set(jnp.asarray(lengths, jnp.int32))

    lengths = jnp.where(number % 4 == 0, named(heavy_load, number // 4), named(usual, number - number // 4 - 1))
    mixed = jax.random.permutation(jax.random.fold_in(own, 3), count)
    giver, receiver = mixed[0:count // 2 * 2:2], mixed[1:count // 2 * 2:2]
    margin = jnp.minimum(lengths[giver] - 1, reach - lengths[receiver]) // 2
    margin = jnp.where((giver == order[0]) | (receiver == order[0]) | (lengths[receiver] == 0), 0, jnp.maximum(margin, 0))
    moved = jax.random.randint(jax.random.fold_in(own, 4), (count // 2,), 0, 1 << 20) % (margin + 1)
    lengths = lengths.at[giver].add(-moved).at[receiver].add(moved)
    members = jnp.searchsorted(jnp.cumsum(lengths), jnp.arange(rows * top), side="right").astype(jnp.int32)
    listing = members.reshape(top, rows).T
    listing = listing[jax.random.permutation(jax.random.fold_in(own, 1), rows)]
    rotation = jax.random.randint(jax.random.fold_in(own, 2), (rows, 1), 0, top)
    return jnp.take_along_axis(listing, (jnp.arange(top)[None, :] + rotation) % top, axis=1)


def shares(count, total, limit, slope, full):
    weights = [(1 << 20) // math.isqrt(grade ** slope) + 1 for grade in range(1, count + 1)]
    largest = limit if full else min(limit, max(-(-total // count), total * weights[0] // sum(weights)))
    least = 1 if total - largest >= count - 1 else 0
    given, spare = [largest] + [least] * (count - 1), total - largest - least * (count - 1)
    while spare > 0:
        candidates = [i for i in range(1, count) if given[i] < largest] or [i for i in range(1, count) if given[i] < limit]
        whole, budget = sum([weights[i] for i in candidates]), spare
        for i in candidates:
            addition = min(limit - given[i], max(1, budget * weights[i] // whole), spare)
            given[i] = given[i] + addition
            spare = spare - addition
    return np.array(given)


def bell_draw(own_key, shape, spread, bound, cuts=(), kind=jnp.bfloat16):
    drawn = spread * jax.random.normal(own_key, shape, jnp.float32)
    if cuts:
        drawn = drawn * level_of(own_key, shape, cuts, -0.22, 0.18)
    return jnp.clip(drawn, -bound, bound).astype(kind)


def setup_inputs(seed: int = 0) -> dict:
    keys = jax.random.split(jax.random.key(seed), 6)
    tokens = bell_draw(keys[0], (TOKENS, D), 1.0, 6.0, ((0, 4), (1, 8)))
    routes_keys = jax.random.split(jax.random.fold_in(keys[1], 1), TOKENS // TOK_E)
    routes_turns = jax.random.permutation(jax.random.fold_in(keys[1], 3), TOKENS // TOK_E)
    routes = jax.vmap(lambda own, number: deal_out(jax.random.fold_in(keys[1], 2), own, number, TOK_E, EXPERTS, TOP, SLOT, 2))(routes_keys, routes_turns).reshape((TOKENS, TOP))
    labels = touch_ends(jax.random.randint(keys[2], (TOKENS,), 0, CLASSES), jax.random.fold_in(keys[2], 1), 0, CLASSES - 1).astype(jnp.int32)
    gate_weight = bell_draw(keys[3], (EXPERTS, D, FF), D ** -0.5, 0.109375, ((0, 4), (2, 8)))
    up_weight = bell_draw(keys[4], (EXPERTS, D, FF), D ** -0.5, 0.109375, ((0, 4), (2, 8)))
    return {"tokens": tokens, "routes": routes, "labels": labels, "gate_weight": gate_weight, "up_weight": up_weight}


def build_rows(routes, labels, tokens, expert):
    hit_mask = jnp.any(routes == expert, axis=1).astype(jnp.int32)
    hit_grid = hit_mask.reshape(N_EXPERT, TOK_E)
    rank_pos = jnp.cumsum(hit_grid, axis=1) - hit_grid
    source_ids = jnp.arange(N_EXPERT, dtype=jnp.int32)[:, None]
    slot_of = jnp.where(hit_grid > 0, source_ids * SLOT + rank_pos, -1).reshape(TOKENS)
    slot_ids = jnp.arange(CAP, dtype=jnp.int32)[:, None]
    selector = slot_ids == slot_of[None, :]
    routed = jnp.dot(selector.astype(jnp.bfloat16), tokens, preferred_element_type=jnp.float32).astype(jnp.bfloat16)
    tag_rows = jnp.sum(jnp.where(selector, labels[None, :] + 1, 0), axis=1).astype(jnp.int32)
    return routed, tag_rows


def reference(tokens, routes, labels, gate_weight, up_weight):
    def per_expert(expert):
        routed, tag_rows = build_rows(routes, labels, tokens, expert)
        gate_pre = jnp.dot(routed, gate_weight[expert], preferred_element_type=jnp.float32)
        up_pre = jnp.dot(routed, up_weight[expert], preferred_element_type=jnp.float32)
        hidden = (jax.nn.silu(gate_pre) * up_pre).astype(jnp.bfloat16)
        live_count = jnp.sum((tag_rows > 0).astype(jnp.float32))
        moment = (jnp.dot(hidden.T, hidden, preferred_element_type=jnp.float32) / live_count).astype(jnp.bfloat16)
        class_ids = jnp.arange(CLASSES, dtype=jnp.int32)
        one_hot = ((tag_rows[:, None] - 1) == class_ids[None, :]).astype(jnp.bfloat16)
        cross_cov = jnp.dot(hidden.T, one_hot, preferred_element_type=jnp.float32) * (CLASSES / live_count)
        return moment, cross_cov

    moments, crosses = lax.map(per_expert, jnp.arange(EXPERTS, dtype=jnp.int32))
    return moments, crosses
```

```python
import functools

import jax
import jax.numpy as jnp
from jax import lax
from jax.experimental import pallas as pl
from jax.experimental.pallas import tpu as pltpu
from jax.sharding import PartitionSpec as P

CLASSES = 16
MIB = 1 << 20
MESH = pl.DeviceIdType.MESH


def gather_kernel(E, B, t_ref, meta_ref, wg_ref, wu_ref, h_ref, m_ref,
                  tok, wg, wu, own, loc_sem, own_sem, tz_s, tsib_s, tpl_s, t_r, m_s, m_r,
                  hsib_s, hup_s, hdn_s, h_r):
    Z = B // 2
    rows, F = t_ref.shape
    W = wg_ref.shape[2]
    e, b = lax.axis_index("expert"), lax.axis_index("blk")
    z, c = b // 2, b % 2
    sib = b + 1 - 2 * c

    g_copy = pltpu.make_async_copy(wg_ref.at[0], wg, loc_sem.at[0])
    u_copy = pltpu.make_async_copy(wu_ref.at[0], wu, loc_sem.at[1])
    g_copy.start()
    u_copy.start()

    barrier = pltpu.get_barrier_semaphore()

    def to(expert, blk):
        return {"expert": expert, "blk": blk}

    def greet(expert, blk):
        pl.semaphore_signal(barrier, inc=1, device_id=to(expert, blk), device_id_type=MESH)

    greet(e, sib)
    for d in range(1, Z):
        greet(e, 2 * lax.rem(z + d, Z) + c)
    for k in range(1, E):
        greet(lax.rem(e + k, E), b)
    pl.semaphore_wait(barrier, Z + E - 1)

    def chunk(s, blk):
        return tok.at[s, :, pl.ds(pl.multiple_of(blk * F, 128), F)]

    def piece(s, blk):
        return h_ref.at[pl.ds(pl.multiple_of(s * rows, rows), rows), pl.ds(pl.multiple_of(blk * W, 128), W)]

    def remote(src, dst, send, recv, expert, blk):
        return pltpu.make_async_remote_copy(
            src_ref=src, dst_ref=dst, send_sem=send, recv_sem=recv,
            device_id=to(expert, blk), device_id_type=MESH)

    def tok_z(d):
        return remote(t_ref, chunk(e, b), tz_s.at[d], t_r.at[e, b], e, 2 * lax.rem(z + d, Z) + c)

    def tok_sib(s, zz, src=None):
        blk = 2 * zz + c
        return remote(chunk(s, blk) if src is None else src, chunk(s, blk), tsib_s.at[s, zz], t_r.at[s, blk], e, sib)

    def tok_plane(k, zz, src=None):
        blk = 2 * zz + c
        return remote(chunk(e, blk) if src is None else src, chunk(e, blk), tpl_s.at[k, zz], t_r.at[e, blk],
                      lax.rem(e + k, E), b)

    def tok_here(s, blk):
        remote(chunk(s, blk), chunk(s, blk), tz_s.at[0], t_r.at[s, blk], e, sib).wait_recv()

    def meta_to(k):
        return remote(meta_ref, m_ref.at[e], m_s.at[k], m_r.at[e], lax.rem(e + k, E), b)

    t_copy = pltpu.make_async_copy(t_ref, chunk(e, b), loc_sem.at[2])
    m_copy = pltpu.make_async_copy(meta_ref, m_ref.at[e], loc_sem.at[3])
    for d in range(1, Z):
        tok_z(d).start()
    tok_sib(e, z, t_ref).start()
    for k in range(1, E):
        tok_plane(k, z, t_ref).start()
    t_copy.start()
    m_copy.start()
    for k in range(1, E):
        meta_to(k).start()

    def h_sib(s, zz, src=None):
        blk = 2 * zz + c
        return remote(piece(s, blk) if src is None else src, piece(s, blk), hsib_s.at[s, zz], h_r.at[s, blk], e, sib)

    def h_up(s, zz, src=None):
        blk = 2 * zz + c
        return remote(piece(s, blk) if src is None else src, piece(s, blk), hup_s.at[s, zz], h_r.at[s, blk], e, b + 2)

    def h_dn(s, zz, src=None):
        blk = 2 * zz + c
        return remote(piece(s, blk) if src is None else src, piece(s, blk), hdn_s.at[s, zz], h_r.at[s, blk], e, b - 2)

    def h_here(s, blk):
        remote(piece(s, blk), piece(s, blk), hsib_s.at[s, 0], h_r.at[s, blk], e, sib).wait_recv()

    def own_copy(s):
        return pltpu.make_async_copy(own.at[s], piece(s, b), own_sem.at[s])

    tile = min(W, 256)

    def compute(j, s):
        @pl.when(j == 0)
        def _():
            def arrived(d, carry):
                zz = lax.rem(z + d, Z)
                tok_here(e, 2 * zz + c)
                tok_sib(e, zz).start()
                for k in range(1, E):
                    tok_plane(k, zz).start()
                return carry

            lax.fori_loop(1, Z, arrived, 0)
            t_copy.wait()
            g_copy.wait()
            u_copy.wait()

        @pl.when(j > 0)
        def _():
            def arrived(d, carry):
                zz = lax.rem(z + d, Z)
                tok_here(s, 2 * zz + c)
                tok_sib(s, zz).start()
                return carry

            lax.fori_loop(0, Z, arrived, 0)

        def other(zz, carry):
            tok_here(s, 2 * zz + 1 - c)
            return carry

        lax.fori_loop(0, Z, other, 0)

        def columns(i, carry):
            cols = pl.ds(pl.multiple_of(i * tile, tile), tile)
            x = tok[s]
            gate = jnp.dot(x, wg[:, cols], preferred_element_type=jnp.float32)
            up = jnp.dot(x, wu[:, cols], preferred_element_type=jnp.float32)
            own[s, :, cols] = (gate / (1.0 + jnp.exp(-gate)) * up).astype(own.dtype)
            return carry

        lax.fori_loop(0, W // tile, columns, 0)

        @pl.when(z < Z - 1)
        def _():
            h_up(s, z, own.at[s]).start()

        @pl.when(z > 0)
        def _():
            h_dn(s, z, own.at[s]).start()

        h_sib(s, z, own.at[s]).start()
        own_copy(s).start()

    def forward(s, d):
        @pl.when(z - d >= 0)
        def _():
            h_here(s, 2 * (z - d) + c)

            @pl.when(z < Z - 1)
            def _():
                h_up(s, z - d).start()

            h_sib(s, z - d).start()

        @pl.when(z + d < Z)
        def _():
            h_here(s, 2 * (z + d) + c)

            @pl.when(z > 0)
            def _():
                h_dn(s, z + d).start()

            h_sib(s, z + d).start()

    def turn(k, carry):
        def inner(i, carry):
            j = E - 1 - i
            s = lax.rem(e + j, E)
            d = k - j

            @pl.when(d == 0)
            def _():
                compute(j, s)

            @pl.when((d > 0) & (d < Z))
            def _():
                forward(s, d)

            return carry

        return lax.fori_loop(0, E, inner, carry)

    lax.fori_loop(0, E + Z - 1, turn, 0)

    m_copy.wait()
    for d in range(1, Z):
        tok_z(d).wait_send()
    for k in range(1, E):
        meta_to(k).wait_send()
        other = lax.rem(e + k, E)
        remote(meta_ref, m_ref.at[other], m_s.at[k], m_r.at[other], other, b).wait_recv()

    def finish(s, carry):
        own_copy(s).wait()

        def chips(zz, carry):
            h_here(s, 2 * zz + 1 - c)
            tok_sib(s, zz).wait_send()
            h_sib(s, zz).wait_send()

            @pl.when(s > 0)
            def _():
                tok_plane(s, zz).wait_send()

            @pl.when((zz <= z) & (z < Z - 1))
            def _():
                h_up(s, zz).wait_send()

            @pl.when((zz >= z) & (z > 0))
            def _():
                h_dn(s, zz).wait_send()

            return carry

        return lax.fori_loop(0, Z, chips, carry)

    lax.fori_loop(0, E, finish, 0)


def gather(tokens, meta, gate_weight, up_weight, E, B):
    rows, F = tokens.shape
    D, W = gate_weight.shape[1:]
    Z = B // 2
    anywhere = pl.BlockSpec(memory_space=pl.ANY)
    dma = pltpu.SemaphoreType.DMA
    return pl.pallas_call(
        functools.partial(gather_kernel, E, B),
        out_shape=[jax.ShapeDtypeStruct((E * rows, B * W), jnp.bfloat16),
                   jax.ShapeDtypeStruct((E,) + meta.shape, jnp.int32)],
        in_specs=[anywhere] * 4,
        out_specs=[anywhere] * 2,
        scratch_shapes=[
            pltpu.VMEM((E, rows, D), jnp.bfloat16),
            pltpu.VMEM((D, W), jnp.bfloat16),
            pltpu.VMEM((D, W), jnp.bfloat16),
            pltpu.VMEM((E, rows, W), jnp.bfloat16),
            dma((4,)), dma((E,)), dma((Z,)), dma((E, Z)), dma((E, Z)), dma((E, B)), dma((E,)), dma((E,)),
            dma((E, Z)), dma((E, Z)), dma((E, Z)), dma((E, B)),
        ],
        compiler_params=pltpu.CompilerParams(
            collective_id=0, has_side_effects=True, vmem_limit_bytes=40 * MIB),
        name="gather_hidden",
    )(tokens, meta, gate_weight, up_weight)


def moment_kernel(E, place, meta_ref, own_ref, all_ref, moment_ref, cross_ref, lhs, scale):
    @pl.when(pl.program_id(0) == 0)
    def _():
        e = place[0]

        def row(i):
            return jnp.concatenate([meta_ref[s, i:i + 1, :] for s in range(E)], axis=1)

        live = (row(0) == e) | (row(1) == e)
        count = jnp.sum(live.astype(jnp.float32), axis=1, keepdims=True)
        flipped = own_ref[...].T
        masked = flipped * live.astype(jnp.bfloat16)
        lhs[...] = masked
        classes = lax.broadcasted_iota(jnp.int32, (CLASSES, live.shape[1]), 0)
        one_hot = ((row(2) == classes) & live).astype(jnp.bfloat16)
        scale[...] = jnp.broadcast_to(1.0 / count, scale.shape)
        cross_ref[...] = lax.dot_general(
            one_hot, masked, (((1,), (1,)), ((), ())), preferred_element_type=jnp.float32) * (CLASSES / count)

    acc = jnp.dot(lhs[...], all_ref[...], preferred_element_type=jnp.float32)
    moment_ref[0] = (acc * scale[0:1, 0:1]).astype(moment_ref.dtype)


def moments(place, meta, hidden, E, B):
    rows, FF = hidden.shape
    W = FF // B
    tile = 512
    return pl.pallas_call(
        functools.partial(moment_kernel, E),
        grid_spec=pltpu.PrefetchScalarGridSpec(
            num_scalar_prefetch=1,
            grid=(FF // tile,),
            in_specs=[
                pl.BlockSpec(meta.shape, lambda i, p: (0, 0, 0)),
                pl.BlockSpec((rows, W), lambda i, p: (0, p[1])),
                pl.BlockSpec((rows, tile), lambda i, p: (0, i)),
            ],
            out_specs=[
                pl.BlockSpec((1, W, tile), lambda i, p: (0, 0, i)),
                pl.BlockSpec((CLASSES, W), lambda i, p: (0, 0)),
            ],
            scratch_shapes=[pltpu.VMEM((W, rows), jnp.bfloat16), pltpu.VMEM((8, 128), jnp.float32)],
        ),
        out_shape=[jax.ShapeDtypeStruct((1, W, FF), jnp.bfloat16), jax.ShapeDtypeStruct((CLASSES, W), jnp.float32)],
        compiler_params=pltpu.CompilerParams(vmem_limit_bytes=40 * MIB),
        name="moments",
    )(place, meta, hidden, hidden)


def plain(tokens, routes, labels, gate_weight, up_weight):
    everyone = lax.all_gather(lax.all_gather(tokens, "expert", axis=0, tiled=True), "blk", axis=1, tiled=True)
    routes = lax.all_gather(routes, "expert", axis=0, tiled=True)
    labels = lax.all_gather(labels, "expert", axis=0, tiled=True)
    live = jnp.any(routes == lax.axis_index("expert"), axis=1)
    gate = jnp.dot(everyone, gate_weight[0], preferred_element_type=jnp.float32)
    up = jnp.dot(everyone, up_weight[0], preferred_element_type=jnp.float32)
    hidden = jnp.where(live[:, None], jax.nn.silu(gate) * up, 0).astype(jnp.bfloat16)
    count = jnp.sum(live.astype(jnp.float32))
    one_hot = (labels[:, None] == jnp.arange(CLASSES, dtype=jnp.int32)[None, :]).astype(jnp.bfloat16)
    over_rows = (((0,), (0,)), ((), ()))
    cross = lax.dot_general(hidden, one_hot, over_rows, preferred_element_type=jnp.float32) * (CLASSES / count)
    full = lax.all_gather(hidden, "blk", axis=1, tiled=True)
    moment = lax.dot_general(hidden, full, over_rows, preferred_element_type=jnp.float32) / count
    return moment.astype(jnp.bfloat16)[None], cross[None]


def shards(tokens, routes, labels, gate_weight, up_weight):
    E, B = lax.axis_size("expert"), lax.axis_size("blk")
    rows, F = tokens.shape
    W = gate_weight.shape[2]
    if B % 2 or F % 128 or W % 256 or rows != 128:
        return plain(tokens, routes, labels, gate_weight, up_weight)
    meta = jnp.concatenate([routes.T, labels[None], jnp.zeros((5, rows), jnp.int32)], axis=0)
    hidden, meta_all = gather(tokens, meta, gate_weight, up_weight, E, B)
    place = jnp.stack([lax.axis_index("expert"), lax.axis_index("blk")]).astype(jnp.int32)
    moment, cross = moments(place, meta_all, hidden, E, B)
    return moment, cross.T[None]


def solution(mesh):
    in_specs = (
        P("expert", "blk"),
        P("expert", None),
        P("expert"),
        P("expert", None, "blk"),
        P("expert", None, "blk"),
    )
    out_specs = (P("expert", "blk", None), P("expert", "blk", None))
    return jax.shard_map(shards, mesh=mesh, in_specs=in_specs, out_specs=out_specs, check_vma=False)
```

```python
import functools

import jax
import jax.numpy as jnp
from jax import lax
from jax.experimental import pallas as pl
from jax.experimental.pallas import tpu as pltpu
from jax.sharding import PartitionSpec as P

CLASSES = 16
MIB = 1 << 20
MESH = pl.DeviceIdType.MESH


def gather_kernel(E, B, t_ref, meta_ref, wg_ref, wu_ref, moment_ref, cross_ref,
                  tok, wg, wu, h_ref, m_ref, lhs, scale, loc_sem, tz_s, tsib_s, tpl_s, t_r, m_s, m_r,
                  hsib_s, hup_s, hdn_s, h_r):
    Z = B // 2
    rows, F = t_ref.shape
    W = wg_ref.shape[2]
    e, b = lax.axis_index("expert"), lax.axis_index("blk")
    z, c = b // 2, b % 2
    sib = b + 1 - 2 * c

    g_copy = pltpu.make_async_copy(wg_ref.at[0], wg, loc_sem.at[0])
    u_copy = pltpu.make_async_copy(wu_ref.at[0], wu, loc_sem.at[1])
    g_copy.start()
    u_copy.start()

    barrier = pltpu.get_barrier_semaphore()

    def to(expert, blk):
        return {"expert": expert, "blk": blk}

    def greet(expert, blk):
        pl.semaphore_signal(barrier, inc=1, device_id=to(expert, blk), device_id_type=MESH)

    greet(e, sib)
    for d in range(1, Z):
        greet(e, 2 * lax.rem(z + d, Z) + c)
    for k in range(1, E):
        greet(lax.rem(e + k, E), b)
    pl.semaphore_wait(barrier, Z + E - 1)

    def chunk(s, blk):
        return tok.at[s, :, pl.ds(pl.multiple_of(blk * F, 128), F)]

    def piece(s, blk):
        return h_ref.at[pl.ds(pl.multiple_of(s * rows, rows), rows), pl.ds(pl.multiple_of(blk * W, 128), W)]

    def remote(src, dst, send, recv, expert, blk):
        return pltpu.make_async_remote_copy(
            src_ref=src, dst_ref=dst, send_sem=send, recv_sem=recv,
            device_id=to(expert, blk), device_id_type=MESH)

    def tok_z(d):
        return remote(t_ref, chunk(e, b), tz_s.at[d], t_r.at[e, b], e, 2 * lax.rem(z + d, Z) + c)

    def tok_sib(s, zz, src=None):
        blk = 2 * zz + c
        return remote(chunk(s, blk) if src is None else src, chunk(s, blk), tsib_s.at[s, zz], t_r.at[s, blk], e, sib)

    def tok_plane(k, zz, src=None):
        blk = 2 * zz + c
        return remote(chunk(e, blk) if src is None else src, chunk(e, blk), tpl_s.at[k, zz], t_r.at[e, blk],
                      lax.rem(e + k, E), b)

    def tok_here(s, blk):
        remote(chunk(s, blk), chunk(s, blk), tz_s.at[0], t_r.at[s, blk], e, sib).wait_recv()

    def meta_to(k):
        return remote(meta_ref, m_ref.at[e], m_s.at[k], m_r.at[e], lax.rem(e + k, E), b)

    t_copy = pltpu.make_async_copy(t_ref, chunk(e, b), loc_sem.at[2])
    m_copy = pltpu.make_async_copy(meta_ref, m_ref.at[e], loc_sem.at[3])
    for d in range(1, Z):
        tok_z(d).start()
    tok_sib(e, z, t_ref).start()
    for k in range(1, E):
        tok_plane(k, z, t_ref).start()
    t_copy.start()
    m_copy.start()
    for k in range(1, E):
        meta_to(k).start()

    def h_sib(s, zz):
        blk = 2 * zz + c
        return remote(piece(s, blk), piece(s, blk), hsib_s.at[s, zz], h_r.at[s, blk], e, sib)

    def h_up(s, zz):
        blk = 2 * zz + c
        return remote(piece(s, blk), piece(s, blk), hup_s.at[s, zz], h_r.at[s, blk], e, b + 2)

    def h_dn(s, zz):
        blk = 2 * zz + c
        return remote(piece(s, blk), piece(s, blk), hdn_s.at[s, zz], h_r.at[s, blk], e, b - 2)

    def h_here(s, blk):
        remote(piece(s, blk), piece(s, blk), hsib_s.at[s, 0], h_r.at[s, blk], e, sib).wait_recv()

    tile = min(W, 256)

    def compute(j, s):
        @pl.when(j == 0)
        def _():
            def arrived(d, carry):
                zz = lax.rem(z + d, Z)
                tok_here(e, 2 * zz + c)
                tok_sib(e, zz).start()
                for k in range(1, E):
                    tok_plane(k, zz).start()
                return carry

            lax.fori_loop(1, Z, arrived, 0)
            t_copy.wait()
            g_copy.wait()
            u_copy.wait()

        @pl.when(j > 0)
        def _():
            def arrived(d, carry):
                zz = lax.rem(z + d, Z)
                tok_here(s, 2 * zz + c)
                tok_sib(s, zz).start()
                return carry

            lax.fori_loop(0, Z, arrived, 0)

        def other(zz, carry):
            tok_here(s, 2 * zz + 1 - c)
            return carry

        lax.fori_loop(0, Z, other, 0)

        def columns(i, carry):
            cols = pl.ds(pl.multiple_of(i * tile, tile), tile)
            x = tok[s]
            gate = jnp.dot(x, wg[:, cols], preferred_element_type=jnp.float32)
            up = jnp.dot(x, wu[:, cols], preferred_element_type=jnp.float32)
            h_ref[pl.ds(pl.multiple_of(s * rows, rows), rows),
                  pl.ds(pl.multiple_of(b * W + i * tile, 128), tile)] = (
                gate / (1.0 + jnp.exp(-gate)) * up).astype(h_ref.dtype)
            return carry

        lax.fori_loop(0, W // tile, columns, 0)

        @pl.when(z < Z - 1)
        def _():
            h_up(s, z).start()

        @pl.when(z > 0)
        def _():
            h_dn(s, z).start()

        h_sib(s, z).start()

    def forward(s, d):
        @pl.when(z - d >= 0)
        def _():
            h_here(s, 2 * (z - d) + c)

            @pl.when(z < Z - 1)
            def _():
                h_up(s, z - d).start()

            h_sib(s, z - d).start()

        @pl.when(z + d < Z)
        def _():
            h_here(s, 2 * (z + d) + c)

            @pl.when(z > 0)
            def _():
                h_dn(s, z + d).start()

            h_sib(s, z + d).start()

    def turn(k, carry):
        def inner(i, carry):
            j = E - 1 - i
            s = lax.rem(e + j, E)
            d = k - j

            @pl.when(d == 0)
            def _():
                compute(j, s)

            @pl.when((d > 0) & (d < Z))
            def _():
                forward(s, d)

            return carry

        lax.fori_loop(0, E, inner, 0)
        d = k - (E - 1)

        @pl.when(d == 0)
        def _():
            prepare()
            block(b)

        @pl.when(d > 0)
        def _():
            @pl.when(z - d >= 0)
            def _():
                block(2 * (z - d) + c)

            @pl.when(z + d < Z)
            def _():
                block(2 * (z + d) + c)

            from_sibling(d - 1)

        return carry

    def prepare():
        m_copy.wait()
        for k in range(1, E):
            meta_to(k).wait_send()
            other = lax.rem(e + k, E)
            remote(meta_ref, m_ref.at[other], m_s.at[k], m_r.at[other], other, b).wait_recv()

        def row(i):
            return jnp.concatenate([m_ref[s, i:i + 1, :] for s in range(E)], axis=1)

        live = (row(0) == e) | (row(1) == e)
        count = jnp.sum(live.astype(jnp.float32), axis=1, keepdims=True)
        masked = h_ref[:, pl.ds(pl.multiple_of(b * W, 128), W)].T * live.astype(jnp.bfloat16)
        lhs[...] = masked
        classes = lax.broadcasted_iota(jnp.int32, (CLASSES, live.shape[1]), 0)
        one_hot = ((row(2) == classes) & live).astype(jnp.bfloat16)
        scale[...] = jnp.broadcast_to(1.0 / count, scale.shape)
        cross_ref[...] = lax.dot_general(
            one_hot, masked, (((1,), (1,)), ((), ())), preferred_element_type=jnp.float32) * (CLASSES / count)

    def block(blk):
        def columns(i, carry):
            cols = pl.ds(pl.multiple_of(blk * W + i * tile, 128), tile)
            acc = jnp.dot(lhs[...], h_ref[:, cols], preferred_element_type=jnp.float32)
            moment_ref[0, :, cols] = (acc * scale[0:1, 0:1]).astype(moment_ref.dtype)
            return carry

        lax.fori_loop(0, W // tile, columns, 0)

    def from_sibling(d):
        def arrived(zz):
            blk = 2 * zz + 1 - c

            def shard(s, carry):
                h_here(s, blk)
                return carry

            lax.fori_loop(0, E, shard, 0)
            block(blk)

        @pl.when(z - d >= 0)
        def _():
            arrived(z - d)

        @pl.when((d > 0) & (z + d < Z))
        def _():
            arrived(z + d)

    lax.fori_loop(0, E + Z - 1, turn, 0)
    from_sibling(Z - 1)

    for d in range(1, Z):
        tok_z(d).wait_send()

    def finish(s, carry):
        def chips(zz, carry):
            tok_sib(s, zz).wait_send()
            h_sib(s, zz).wait_send()

            @pl.when(s > 0)
            def _():
                tok_plane(s, zz).wait_send()

            @pl.when((zz <= z) & (z < Z - 1))
            def _():
                h_up(s, zz).wait_send()

            @pl.when((zz >= z) & (z > 0))
            def _():
                h_dn(s, zz).wait_send()

            return carry

        return lax.fori_loop(0, Z, chips, carry)

    lax.fori_loop(0, E, finish, 0)


def gather(tokens, meta, gate_weight, up_weight, E, B):
    rows, F = tokens.shape
    D, W = gate_weight.shape[1:]
    Z = B // 2
    in_hbm = pl.BlockSpec(memory_space=pltpu.HBM)
    in_vmem = pl.BlockSpec(memory_space=pltpu.VMEM)
    dma = pltpu.SemaphoreType.DMA
    return pl.pallas_call(
        functools.partial(gather_kernel, E, B),
        out_shape=[pltpu.VMEM((1, W, B * W), jnp.bfloat16), jax.ShapeDtypeStruct((CLASSES, W), jnp.float32)],
        in_specs=[in_hbm, in_vmem, in_hbm, in_hbm],
        out_specs=[in_vmem, in_vmem],
        scratch_shapes=[
            pltpu.VMEM((E, rows, D), jnp.bfloat16),
            pltpu.VMEM((D, W), jnp.bfloat16),
            pltpu.VMEM((D, W), jnp.bfloat16),
            pltpu.VMEM((E * rows, B * W), jnp.bfloat16),
            pltpu.VMEM((E,) + meta.shape, jnp.int32),
            pltpu.VMEM((W, E * rows), jnp.bfloat16),
            pltpu.VMEM((8, 128), jnp.float32),
            dma((4,)), dma((Z,)), dma((E, Z)), dma((E, Z)), dma((E, B)), dma((E,)), dma((E,)),
            dma((E, Z)), dma((E, Z)), dma((E, Z)), dma((E, B)),
        ],
        compiler_params=pltpu.CompilerParams(
            collective_id=0, has_side_effects=True, vmem_limit_bytes=44 * MIB),
        name="hidden_moments",
    )(tokens, meta, gate_weight, up_weight)


def plain(tokens, routes, labels, gate_weight, up_weight):
    everyone = lax.all_gather(lax.all_gather(tokens, "expert", axis=0, tiled=True), "blk", axis=1, tiled=True)
    routes = lax.all_gather(routes, "expert", axis=0, tiled=True)
    labels = lax.all_gather(labels, "expert", axis=0, tiled=True)
    live = jnp.any(routes == lax.axis_index("expert"), axis=1)
    gate = jnp.dot(everyone, gate_weight[0], preferred_element_type=jnp.float32)
    up = jnp.dot(everyone, up_weight[0], preferred_element_type=jnp.float32)
    hidden = jnp.where(live[:, None], jax.nn.silu(gate) * up, 0).astype(jnp.bfloat16)
    count = jnp.sum(live.astype(jnp.float32))
    one_hot = (labels[:, None] == jnp.arange(CLASSES, dtype=jnp.int32)[None, :]).astype(jnp.bfloat16)
    over_rows = (((0,), (0,)), ((), ()))
    cross = lax.dot_general(hidden, one_hot, over_rows, preferred_element_type=jnp.float32) * (CLASSES / count)
    full = lax.all_gather(hidden, "blk", axis=1, tiled=True)
    moment = lax.dot_general(hidden, full, over_rows, preferred_element_type=jnp.float32) / count
    return moment.astype(jnp.bfloat16)[None], cross[None]


def shards(tokens, routes, labels, gate_weight, up_weight):
    E, B = lax.axis_size("expert"), lax.axis_size("blk")
    rows, F = tokens.shape
    W = gate_weight.shape[2]
    if B % 2 or F % 128 or W % 256 or rows != 128:
        return plain(tokens, routes, labels, gate_weight, up_weight)
    meta = jnp.concatenate([routes.T, labels[None], jnp.zeros((5, rows), jnp.int32)], axis=0)
    moment, cross = gather(tokens, meta, gate_weight, up_weight, E, B)
    return moment, cross.T[None]


def solution(mesh):
    in_specs = (
        P("expert", "blk"),
        P("expert", None),
        P("expert"),
        P("expert", None, "blk"),
        P("expert", None, "blk"),
    )
    out_specs = (P("expert", "blk", None), P("expert", "blk", None))
    return jax.shard_map(shards, mesh=mesh, in_specs=in_specs, out_specs=out_specs, check_vma=False)
```

```python
import functools

import jax
import jax.numpy as jnp
from jax import lax
from jax.experimental import pallas as pl
from jax.experimental.pallas import tpu as pltpu
from jax.sharding import PartitionSpec as P

CLASSES = 16
MIB = 1 << 20
MESH = pl.DeviceIdType.MESH


def gather_kernel(E, B, t_ref, meta_ref, rc_ref, wg_ref, wu_ref, moment_ref, cross_ref,
                  tok, wg, wu, h_ref, m_ref, lhs, scale, loc_sem, tz_s, tsib_s, tpl_s, t_r, m_s, m_r,
                  hsib_s, hup_s, hdn_s, h_r,
                  mk, g_buf, pq, r_buf, fw_s, fw_r, pqup_s, pqdn_s, pq_r, rp_s, wsib_s, w_r):
    Z = B // 2
    rows, F = t_ref.shape
    W = wg_ref.shape[2]
    V = W // 2
    e, b = lax.axis_index("expert"), lax.axis_index("blk")
    z, c = b // 2, b % 2
    sib = b + 1 - 2 * c

    g_copy = pltpu.make_async_copy(wg_ref.at[0], wg, loc_sem.at[0])
    u_copy = pltpu.make_async_copy(wu_ref.at[0], wu, loc_sem.at[1])
    g_copy.start()
    u_copy.start()

    barrier = pltpu.get_barrier_semaphore()

    def to(expert, blk):
        return {"expert": expert, "blk": blk}

    def greet(expert, blk):
        pl.semaphore_signal(barrier, inc=1, device_id=to(expert, blk), device_id_type=MESH)

    greet(e, sib)
    for d in range(1, Z):
        greet(e, 2 * lax.rem(z + d, Z) + c)
    for k in range(1, E):
        greet(lax.rem(e + k, E), b)
    pl.semaphore_wait(barrier, Z + E - 1)

    def chunk(s, blk):
        return tok.at[s, :, pl.ds(pl.multiple_of(blk * F, 128), F)]

    def part(s, blk, start, width):
        return h_ref.at[pl.ds(pl.multiple_of(s * rows, rows), rows),
                        pl.ds(pl.multiple_of(blk * W + start, 128), width)]

    def piece(s, blk):
        return part(s, blk, 0, V)

    def rest(s, blk):
        return part(s, blk, V, W - V)

    def remote(src, dst, send, recv, expert, blk):
        return pltpu.make_async_remote_copy(
            src_ref=src, dst_ref=dst, send_sem=send, recv_sem=recv,
            device_id=to(expert, blk), device_id_type=MESH)

    def tok_z(d):
        return remote(t_ref, chunk(e, b), tz_s.at[d], t_r.at[e, b], e, 2 * lax.rem(z + d, Z) + c)

    def tok_sib(s, zz, src=None):
        blk = 2 * zz + c
        return remote(chunk(s, blk) if src is None else src, chunk(s, blk), tsib_s.at[s, zz], t_r.at[s, blk], e, sib)

    def tok_plane(k, zz, src=None):
        blk = 2 * zz + c
        return remote(chunk(e, blk) if src is None else src, chunk(e, blk), tpl_s.at[k, zz], t_r.at[e, blk],
                      lax.rem(e + k, E), b)

    def tok_here(s, blk):
        remote(chunk(s, blk), chunk(s, blk), tz_s.at[0], t_r.at[s, blk], e, sib).wait_recv()

    def meta_to(k):
        return remote(meta_ref, m_ref.at[e], m_s.at[k], m_r.at[e], lax.rem(e + k, E), b)

    t_copy = pltpu.make_async_copy(t_ref, chunk(e, b), loc_sem.at[2])
    m_copy = pltpu.make_async_copy(meta_ref, m_ref.at[e], loc_sem.at[3])
    for d in range(1, Z):
        tok_z(d).start()
    tok_sib(e, z, t_ref).start()
    for k in range(1, E):
        tok_plane(k, z, t_ref).start()
    t_copy.start()
    m_copy.start()
    for k in range(1, E):
        meta_to(k).start()

    def h_sib(s, zz):
        blk = 2 * zz + c
        return remote(piece(s, blk), piece(s, blk), hsib_s.at[s, zz], h_r.at[s, blk], e, sib)

    def own_sib(s, core):
        blk = 2 * z + core
        return remote(part(s, blk, 0, W), part(s, blk, 0, W), hsib_s.at[s, z], h_r.at[s, blk], e, sib)

    def meet(s):
        return remote(rest(s, b), g_buf.at[e], fw_s.at[s], fw_r.at[e], s, b)

    def pq_up(zz):
        return remote(pq.at[zz], pq.at[zz], pqup_s.at[zz], pq_r.at[zz], e, b + 2)

    def pq_dn(zz):
        return remote(pq.at[zz], pq.at[zz], pqdn_s.at[zz], pq_r.at[zz], e, b - 2)

    def deal(k, zz):
        blk = 2 * zz + c
        return remote(r_buf.at[zz, k], rest(e, blk), rp_s.at[k, zz], w_r.at[e, blk], lax.rem(e + k, E), b)

    def w_sib(s, zz):
        blk = 2 * zz + c
        return remote(rest(s, blk), rest(s, blk), wsib_s.at[s, zz], w_r.at[s, blk], e, sib)

    def w_here(s, blk):
        remote(rest(s, blk), rest(s, blk), wsib_s.at[s, 0], w_r.at[s, blk], e, sib).wait_recv()

    def pass_on(zz):
        @pl.when((zz <= z) & (z < Z - 1))
        def _():
            pq_up(zz).start()

        @pl.when((zz >= z) & (z > 0))
        def _():
            pq_dn(zz).start()

    def pick():
        for k in range(1, E):
            other = lax.rem(e + k, E)
            remote(rest(e, b), g_buf.at[other], fw_s.at[other], fw_r.at[other], other, b).wait_recv()

        def lanes(i, carry):
            cols = pl.ds(pl.multiple_of(i * 128, 128), 128)
            mine = h_ref[pl.ds(pl.multiple_of(e * rows, rows), rows),
                         pl.ds(pl.multiple_of(b * W + V + i * 128, 128), 128)]
            for top in range(2):
                total = mine * mk[top, e]
                for k in range(1, E):
                    other = lax.rem(e + k, E)
                    total += g_buf[other, :, cols] * mk[top, other]
                pq[z, top, :, cols] = total
            return carry

        lax.fori_loop(0, (W - V) // 128, lanes, 0)
        pass_on(z)

    def unpick(zz):
        remote(pq.at[zz], pq.at[zz], pqup_s.at[zz], pq_r.at[zz], e, sib).wait_recv()
        pass_on(zz)
        blk = 2 * zz + c

        def lanes(i, carry):
            cols = pl.ds(pl.multiple_of(i * 128, 128), 128)
            first, second = pq[zz, 0, :, cols], pq[zz, 1, :, cols]
            for k in range(E):
                other = lax.rem(e + k, E)
                value = first * mk[0, other] + second * mk[1, other]
                if k:
                    r_buf[zz, k, :, cols] = value
                else:
                    h_ref[pl.ds(pl.multiple_of(e * rows, rows), rows),
                          pl.ds(pl.multiple_of(blk * W + V + i * 128, 128), 128)] = value
            return carry

        lax.fori_loop(0, (W - V) // 128, lanes, 0)
        for k in range(1, E):
            deal(k, zz).start()
        w_sib(e, zz).start()

    def dealt(zz):
        for k in range(1, E):
            s = lax.rem(e + k, E)
            w_here(s, 2 * zz + c)
            w_sib(s, zz).start()

    def both(d, action):
        @pl.when((d > 0) & (d < Z) & (z - d >= 0))
        def _():
            action(z - d)

        @pl.when((d > 0) & (z + d < Z))
        def _():
            action(z + d)

    for top in range(2):
        for k in range(E):
            mk[top, k] = (rc_ref[top] == k).astype(mk.dtype)

    def h_up(s, zz):
        blk = 2 * zz + c
        return remote(piece(s, blk), piece(s, blk), hup_s.at[s, zz], h_r.at[s, blk], e, b + 2)

    def h_dn(s, zz):
        blk = 2 * zz + c
        return remote(piece(s, blk), piece(s, blk), hdn_s.at[s, zz], h_r.at[s, blk], e, b - 2)

    def h_here(s, blk):
        remote(piece(s, blk), piece(s, blk), hsib_s.at[s, 0], h_r.at[s, blk], e, sib).wait_recv()

    tile = min(W, 256)

    def compute(j, s):
        @pl.when(j == 0)
        def _():
            def arrived(d, carry):
                zz = lax.rem(z + d, Z)
                tok_here(e, 2 * zz + c)
                tok_sib(e, zz).start()
                for k in range(1, E):
                    tok_plane(k, zz).start()
                return carry

            lax.fori_loop(1, Z, arrived, 0)
            t_copy.wait()
            g_copy.wait()
            u_copy.wait()

        @pl.when(j > 0)
        def _():
            def arrived(d, carry):
                zz = lax.rem(z + d, Z)
                tok_here(s, 2 * zz + c)
                tok_sib(s, zz).start()
                return carry

            lax.fori_loop(0, Z, arrived, 0)

        def other(zz, carry):
            tok_here(s, 2 * zz + 1 - c)
            return carry

        lax.fori_loop(0, Z, other, 0)

        def columns(i, carry):
            cols = pl.ds(pl.multiple_of(i * tile, tile), tile)
            x = tok[s]
            gate = jnp.dot(x, wg[:, cols], preferred_element_type=jnp.float32)
            up = jnp.dot(x, wu[:, cols], preferred_element_type=jnp.float32)
            h_ref[pl.ds(pl.multiple_of(s * rows, rows), rows),
                  pl.ds(pl.multiple_of(b * W + i * tile, 128), tile)] = (
                gate / (1.0 + jnp.exp(-gate)) * up).astype(h_ref.dtype)
            return carry

        lax.fori_loop(0, W // tile, columns, 0)

        @pl.when(z < Z - 1)
        def _():
            h_up(s, z).start()

        @pl.when(z > 0)
        def _():
            h_dn(s, z).start()

        own_sib(s, c).start()

        @pl.when(j > 0)
        def _():
            meet(s).start()

    def forward(s, d):
        @pl.when(z - d >= 0)
        def _():
            h_here(s, 2 * (z - d) + c)

            @pl.when(z < Z - 1)
            def _():
                h_up(s, z - d).start()

            h_sib(s, z - d).start()

        @pl.when(z + d < Z)
        def _():
            h_here(s, 2 * (z + d) + c)

            @pl.when(z > 0)
            def _():
                h_dn(s, z + d).start()

            h_sib(s, z + d).start()

    def turn(k, carry):
        def inner(i, carry):
            j = E - 1 - i
            s = lax.rem(e + j, E)
            d = k - j

            @pl.when(d == 0)
            def _():
                compute(j, s)

            @pl.when((d > 0) & (d < Z))
            def _():
                forward(s, d)

            return carry

        lax.fori_loop(0, E, inner, 0)
        d = k - (E - 1)

        @pl.when(d == 0)
        def _():
            pick()
            prepare()
            block(b, 0, W)

        @pl.when(d > 0)
        def _():
            both(d, unpick)
            both(d - 1, dealt)
            both(d, lambda zz: block(2 * zz + c, 0, V))

            @pl.when(d == 1)
            def _():
                def shard(s, carry):
                    own_sib(s, 1 - c).wait_recv()
                    return carry

                lax.fori_loop(0, E, shard, 0)
                block(2 * z + 1 - c, 0, W)

            both(d - 1, whole_from_sibling)
            both(d - 1, lambda zz: block(2 * zz + c, V, W))
            both(d - 2, rest_from_sibling)

        return carry

    def prepare():
        m_copy.wait()
        for k in range(1, E):
            meta_to(k).wait_send()
            other = lax.rem(e + k, E)
            remote(meta_ref, m_ref.at[other], m_s.at[k], m_r.at[other], other, b).wait_recv()

        def row(i):
            return jnp.concatenate([m_ref[s, i:i + 1, :] for s in range(E)], axis=1)

        live = (row(0) == e) | (row(1) == e)
        count = jnp.sum(live.astype(jnp.float32), axis=1, keepdims=True)
        masked = h_ref[:, pl.ds(pl.multiple_of(b * W, 128), W)].T * live.astype(jnp.bfloat16)
        lhs[...] = masked
        classes = lax.broadcasted_iota(jnp.int32, (CLASSES, live.shape[1]), 0)
        one_hot = ((row(2) == classes) & live).astype(jnp.bfloat16)
        scale[...] = jnp.broadcast_to(1.0 / count, scale.shape)
        cross_ref[...] = lax.dot_general(
            one_hot, masked, (((1,), (1,)), ((), ())), preferred_element_type=jnp.float32) * (CLASSES / count)

    def block(blk, start, stop):
        def columns(i, carry):
            cols = pl.ds(pl.multiple_of(blk * W + i * tile, 128), tile)
            acc = jnp.dot(lhs[...], h_ref[:, cols], preferred_element_type=jnp.float32)
            moment_ref[0, :, cols] = (acc * scale[0:1, 0:1]).astype(moment_ref.dtype)
            return carry

        lax.fori_loop(start // tile, stop // tile, columns, 0)

    def whole_from_sibling(zz):
        def shard(s, carry):
            h_here(s, 2 * zz + 1 - c)
            return carry

        lax.fori_loop(0, E, shard, 0)
        block(2 * zz + 1 - c, 0, V)

    def rest_from_sibling(zz):
        def shard(s, carry):
            w_here(s, 2 * zz + 1 - c)
            return carry

        lax.fori_loop(0, E, shard, 0)
        block(2 * zz + 1 - c, V, W)

    lax.fori_loop(0, E + Z + 1, turn, 0)

    for d in range(1, Z):
        tok_z(d).wait_send()

    def finish(s, carry):
        def chips(zz, carry):
            tok_sib(s, zz).wait_send()

            @pl.when(zz == z)
            def _():
                own_sib(s, c).wait_send()

            @pl.when(zz != z)
            def _():
                h_sib(s, zz).wait_send()
                w_sib(s, zz).wait_send()

            @pl.when((zz != z) & (s > 0))
            def _():
                deal(s, zz).wait_send()

            @pl.when(s > 0)
            def _():
                tok_plane(s, zz).wait_send()

            @pl.when((zz <= z) & (z < Z - 1))
            def _():
                h_up(s, zz).wait_send()

            @pl.when((zz >= z) & (z > 0))
            def _():
                h_dn(s, zz).wait_send()

            return carry

        return lax.fori_loop(0, Z, chips, carry)

    lax.fori_loop(0, E, finish, 0)
    for k in range(1, E):
        meet(lax.rem(e + k, E)).wait_send()

    def lines(zz, carry):
        @pl.when((zz <= z) & (z < Z - 1))
        def _():
            pq_up(zz).wait_send()

        @pl.when((zz >= z) & (z > 0))
        def _():
            pq_dn(zz).wait_send()

        return carry

    lax.fori_loop(0, Z, lines, 0)


def gather(tokens, meta, columns, gate_weight, up_weight, E, B):
    rows, F = tokens.shape
    D, W = gate_weight.shape[1:]
    Z = B // 2
    in_hbm = pl.BlockSpec(memory_space=pltpu.HBM)
    in_vmem = pl.BlockSpec(memory_space=pltpu.VMEM)
    dma = pltpu.SemaphoreType.DMA
    return pl.pallas_call(
        functools.partial(gather_kernel, E, B),
        out_shape=[pltpu.VMEM((1, W, B * W), jnp.bfloat16), jax.ShapeDtypeStruct((CLASSES, W), jnp.float32)],
        in_specs=[in_hbm, in_vmem, in_vmem, in_hbm, in_hbm],
        out_specs=[in_vmem, in_vmem],
        scratch_shapes=[
            pltpu.VMEM((E, rows, D), jnp.bfloat16),
            pltpu.VMEM((D, W), jnp.bfloat16),
            pltpu.VMEM((D, W), jnp.bfloat16),
            pltpu.VMEM((E * rows, B * W), jnp.bfloat16),
            pltpu.VMEM((E,) + meta.shape, jnp.int32),
            pltpu.VMEM((W, E * rows), jnp.bfloat16),
            pltpu.VMEM((8, 128), jnp.float32),
            dma((4,)), dma((Z,)), dma((E, Z)), dma((E, Z)), dma((E, B)), dma((E,)), dma((E,)),
            dma((E, Z)), dma((E, Z)), dma((E, Z)), dma((E, B)),
            pltpu.VMEM((2, E, rows, 128), jnp.bfloat16),
            pltpu.VMEM((E, rows, W // 2), jnp.bfloat16),
            pltpu.VMEM((Z, 2, rows, W // 2), jnp.bfloat16),
            pltpu.VMEM((Z, E, rows, W // 2), jnp.bfloat16),
            dma((E,)), dma((E,)), dma((Z,)), dma((Z,)), dma((Z,)), dma((E, Z)), dma((E, Z)), dma((E, B)),
        ],
        compiler_params=pltpu.CompilerParams(
            collective_id=0, has_side_effects=True, vmem_limit_bytes=44 * MIB),
        name="hidden_moments",
    )(tokens, meta, columns, gate_weight, up_weight)


def plain(tokens, routes, labels, gate_weight, up_weight):
    everyone = lax.all_gather(lax.all_gather(tokens, "expert", axis=0, tiled=True), "blk", axis=1, tiled=True)
    routes = lax.all_gather(routes, "expert", axis=0, tiled=True)
    labels = lax.all_gather(labels, "expert", axis=0, tiled=True)
    live = jnp.any(routes == lax.axis_index("expert"), axis=1)
    gate = jnp.dot(everyone, gate_weight[0], preferred_element_type=jnp.float32)
    up = jnp.dot(everyone, up_weight[0], preferred_element_type=jnp.float32)
    hidden = jnp.where(live[:, None], jax.nn.silu(gate) * up, 0).astype(jnp.bfloat16)
    count = jnp.sum(live.astype(jnp.float32))
    one_hot = (labels[:, None] == jnp.arange(CLASSES, dtype=jnp.int32)[None, :]).astype(jnp.bfloat16)
    over_rows = (((0,), (0,)), ((), ()))
    cross = lax.dot_general(hidden, one_hot, over_rows, preferred_element_type=jnp.float32) * (CLASSES / count)
    full = lax.all_gather(hidden, "blk", axis=1, tiled=True)
    moment = lax.dot_general(hidden, full, over_rows, preferred_element_type=jnp.float32) / count
    return moment.astype(jnp.bfloat16)[None], cross[None]


def shards(tokens, routes, labels, gate_weight, up_weight):
    E, B = lax.axis_size("expert"), lax.axis_size("blk")
    rows, F = tokens.shape
    W = gate_weight.shape[2]
    if B % 2 or F % 128 or W % 512 or rows != 128 or routes.shape[1] != 2:
        return plain(tokens, routes, labels, gate_weight, up_weight)
    meta = jnp.concatenate([routes.T, labels[None], jnp.zeros((5, rows), jnp.int32)], axis=0)
    columns = jnp.broadcast_to(routes.T[:, :, None], routes.T.shape + (128,))
    moment, cross = gather(tokens, meta, columns, gate_weight, up_weight, E, B)
    return moment, cross.T[None]


def solution(mesh):
    in_specs = (
        P("expert", "blk"),
        P("expert", None),
        P("expert"),
        P("expert", None, "blk"),
        P("expert", None, "blk"),
    )
    out_specs = (P("expert", "blk", None), P("expert", "blk", None))
    return jax.shard_map(shards, mesh=mesh, in_specs=in_specs, out_specs=out_specs, check_vma=False)
```

```python
import functools

import jax
import jax.numpy as jnp
from jax import lax
from jax.experimental import pallas as pl
from jax.experimental.pallas import tpu as pltpu
from jax.sharding import PartitionSpec as P

CLASSES = 16
MIB = 1 << 20
MESH = pl.DeviceIdType.MESH


def gather_kernel(E, B, t_ref, meta_ref, rc_ref, wg_ref, wu_ref, moment_ref, cross_ref,
                  tok, wg, wu, h_ref, m_ref, lhs, scale, loc_sem, tz_s, tsib_s, tpl_s, t_r, m_s, m_r,
                  hsib_s, hup_s, hdn_s, h_r,
                  mk, g_buf, pq, r_buf, fw_s, fw_r, pqup_s, pqdn_s, pq_r, rp_s, wsib_s, w_r):
    Z = B // 2
    rows, F = t_ref.shape
    W = wg_ref.shape[2]
    V = W // 2
    e, b = lax.axis_index("expert"), lax.axis_index("blk")
    z, c = b // 2, b % 2
    sib = b + 1 - 2 * c

    def mate(k):
        if E == 4:
            return 2 * lax.rem(e // 2 + k // 2, 2) + lax.rem(e % 2 + k % 2, 2)
        return lax.rem(e + k, E)

    g_copy = pltpu.make_async_copy(wg_ref.at[0], wg, loc_sem.at[0])
    u_copy = pltpu.make_async_copy(wu_ref.at[0], wu, loc_sem.at[1])
    g_copy.start()
    u_copy.start()

    barrier = pltpu.get_barrier_semaphore()

    def to(expert, blk):
        return {"expert": expert, "blk": blk}

    def greet(expert, blk):
        pl.semaphore_signal(barrier, inc=1, device_id=to(expert, blk), device_id_type=MESH)

    greet(e, sib)
    for d in range(1, Z):
        greet(e, 2 * lax.rem(z + d, Z) + c)
    for k in range(1, E):
        greet(mate(k), b)
    pl.semaphore_wait(barrier, Z + E - 1)

    def chunk(s, blk):
        return tok.at[s, :, pl.ds(pl.multiple_of(blk * F, 128), F)]

    def part(s, blk, start, width):
        return h_ref.at[pl.ds(pl.multiple_of(s * rows, rows), rows),
                        pl.ds(pl.multiple_of(blk * W + start, 128), width)]

    def piece(s, blk):
        return part(s, blk, 0, V)

    def rest(s, blk):
        return part(s, blk, V, W - V)

    def remote(src, dst, send, recv, expert, blk):
        return pltpu.make_async_remote_copy(
            src_ref=src, dst_ref=dst, send_sem=send, recv_sem=recv,
            device_id=to(expert, blk), device_id_type=MESH)

    def tok_z(d):
        return remote(t_ref, chunk(e, b), tz_s.at[d], t_r.at[e, b], e, 2 * lax.rem(z + d, Z) + c)

    def tok_sib(s, zz, src=None):
        blk = 2 * zz + c
        return remote(chunk(s, blk) if src is None else src, chunk(s, blk), tsib_s.at[s, zz], t_r.at[s, blk], e, sib)

    def tok_plane(k, zz, src=None):
        blk = 2 * zz + c
        return remote(chunk(e, blk) if src is None else src, chunk(e, blk), tpl_s.at[k, zz], t_r.at[e, blk],
                      mate(k), b)

    def tok_here(s, blk):
        remote(chunk(s, blk), chunk(s, blk), tz_s.at[0], t_r.at[s, blk], e, sib).wait_recv()

    def meta_to(k):
        return remote(meta_ref, m_ref.at[e], m_s.at[k], m_r.at[e], mate(k), b)

    t_copy = pltpu.make_async_copy(t_ref, chunk(e, b), loc_sem.at[2])
    m_copy = pltpu.make_async_copy(meta_ref, m_ref.at[e], loc_sem.at[3])
    for d in range(1, Z):
        tok_z(d).start()
    tok_sib(e, z, t_ref).start()
    for k in range(1, E - 1):
        tok_plane(k, z, t_ref).start()
    t_copy.start()
    m_copy.start()
    for k in range(1, E):
        meta_to(k).start()

    def h_sib(s, zz):
        blk = 2 * zz + c
        return remote(piece(s, blk), piece(s, blk), hsib_s.at[s, zz], h_r.at[s, blk], e, sib)

    def own_sib(s, core):
        blk = 2 * z + core
        return remote(part(s, blk, 0, W), part(s, blk, 0, W), hsib_s.at[s, z], h_r.at[s, blk], e, sib)

    def meet(s):
        return remote(rest(s, b), g_buf.at[e], fw_s.at[s], fw_r.at[e], s, b)

    def pq_up(zz):
        return remote(pq.at[zz], pq.at[zz], pqup_s.at[zz], pq_r.at[zz], e, b + 2)

    def pq_dn(zz):
        return remote(pq.at[zz], pq.at[zz], pqdn_s.at[zz], pq_r.at[zz], e, b - 2)

    def deal(k, zz):
        blk = 2 * zz + c
        return remote(r_buf.at[zz, k], rest(e, blk), rp_s.at[k, zz], w_r.at[e, blk], mate(k), b)

    def w_sib(s, zz):
        blk = 2 * zz + c
        return remote(rest(s, blk), rest(s, blk), wsib_s.at[s, zz], w_r.at[s, blk], e, sib)

    def w_here(s, blk):
        remote(rest(s, blk), rest(s, blk), wsib_s.at[s, 0], w_r.at[s, blk], e, sib).wait_recv()

    def pass_on(zz):
        @pl.when((zz <= z) & (z < Z - 1))
        def _():
            pq_up(zz).start()

        @pl.when((zz >= z) & (z > 0))
        def _():
            pq_dn(zz).start()

    def pick():
        for k in range(1, E):
            other = mate(k)
            remote(rest(e, b), g_buf.at[other], fw_s.at[other], fw_r.at[other], other, b).wait_recv()

        def lanes(i, carry):
            cols = pl.ds(pl.multiple_of(i * 128, 128), 128)
            mine = h_ref[pl.ds(pl.multiple_of(e * rows, rows), rows),
                         pl.ds(pl.multiple_of(b * W + V + i * 128, 128), 128)]
            for top in range(2):
                total = mine * mk[top, e]
                for k in range(1, E):
                    other = mate(k)
                    total += g_buf[other, :, cols] * mk[top, other]
                pq[z, top, :, cols] = total
            return carry

        lax.fori_loop(0, (W - V) // 128, lanes, 0)
        pass_on(z)

    def unpick(zz):
        remote(pq.at[zz], pq.at[zz], pqup_s.at[zz], pq_r.at[zz], e, sib).wait_recv()
        pass_on(zz)
        blk = 2 * zz + c

        def lanes(i, carry):
            cols = pl.ds(pl.multiple_of(i * 128, 128), 128)
            first, second = pq[zz, 0, :, cols], pq[zz, 1, :, cols]
            for k in range(E):
                other = mate(k)
                value = first * mk[0, other] + second * mk[1, other]
                if k:
                    r_buf[zz, k, :, cols] = value
                else:
                    h_ref[pl.ds(pl.multiple_of(e * rows, rows), rows),
                          pl.ds(pl.multiple_of(blk * W + V + i * 128, 128), 128)] = value
            return carry

        lax.fori_loop(0, (W - V) // 128, lanes, 0)
        for k in range(1, E):
            deal(k, zz).start()
        w_sib(e, zz).start()

    def dealt(zz):
        for k in range(1, E):
            s = mate(k)
            w_here(s, 2 * zz + c)
            w_sib(s, zz).start()

    def both(d, action):
        @pl.when((d > 0) & (d < Z) & (z - d >= 0))
        def _():
            action(z - d)

        @pl.when((d > 0) & (z + d < Z))
        def _():
            action(z + d)

    for top in range(2):
        for k in range(E):
            mk[top, k] = (rc_ref[top] == k).astype(mk.dtype)

    def h_up(s, zz):
        blk = 2 * zz + c
        return remote(piece(s, blk), piece(s, blk), hup_s.at[s, zz], h_r.at[s, blk], e, b + 2)

    def h_dn(s, zz):
        blk = 2 * zz + c
        return remote(piece(s, blk), piece(s, blk), hdn_s.at[s, zz], h_r.at[s, blk], e, b - 2)

    def h_here(s, blk):
        remote(piece(s, blk), piece(s, blk), hsib_s.at[s, 0], h_r.at[s, blk], e, sib).wait_recv()

    tile = min(W, 256)

    def compute(j, s):
        @pl.when(j == 0)
        def _():
            def arrived(d, carry):
                zz = lax.rem(z + d, Z)
                tok_here(e, 2 * zz + c)
                tok_sib(e, zz).start()
                for k in range(1, E - 1):
                    tok_plane(k, zz).start()
                return carry

            lax.fori_loop(1, Z, arrived, 0)
            t_copy.wait()

            def across(zz, carry):
                tok_plane(E - 1, zz).start()
                return carry

            lax.fori_loop(0, Z, across, 0)
            g_copy.wait()
            u_copy.wait()

        @pl.when(j > 0)
        def _():
            def arrived(d, carry):
                zz = lax.rem(z + d, Z)
                tok_here(s, 2 * zz + c)
                tok_sib(s, zz).start()
                return carry

            lax.fori_loop(0, Z, arrived, 0)

        def other(zz, carry):
            tok_here(s, 2 * zz + 1 - c)
            return carry

        lax.fori_loop(0, Z, other, 0)

        def columns(i, carry):
            cols = pl.ds(pl.multiple_of(i * tile, tile), tile)
            x = tok[s]
            gate = jnp.dot(x, wg[:, cols], preferred_element_type=jnp.float32)
            up = jnp.dot(x, wu[:, cols], preferred_element_type=jnp.float32)
            h_ref[pl.ds(pl.multiple_of(s * rows, rows), rows),
                  pl.ds(pl.multiple_of(b * W + i * tile, 128), tile)] = (
                gate / (1.0 + jnp.exp(-gate)) * up).astype(h_ref.dtype)
            return carry

        lax.fori_loop(0, W // tile, columns, 0)

        @pl.when(z < Z - 1)
        def _():
            h_up(s, z).start()

        @pl.when(z > 0)
        def _():
            h_dn(s, z).start()

        own_sib(s, c).start()

        @pl.when(j > 0)
        def _():
            meet(s).start()

    def forward(s, d):
        @pl.when(z - d >= 0)
        def _():
            h_here(s, 2 * (z - d) + c)

            @pl.when(z < Z - 1)
            def _():
                h_up(s, z - d).start()

            h_sib(s, z - d).start()

        @pl.when(z + d < Z)
        def _():
            h_here(s, 2 * (z + d) + c)

            @pl.when(z > 0)
            def _():
                h_dn(s, z + d).start()

            h_sib(s, z + d).start()

    def turn(k, carry):
        def inner(i, carry):
            j = E - 1 - i
            s = mate(j)
            d = k - j

            @pl.when(d == 0)
            def _():
                compute(j, s)

            @pl.when((d > 0) & (d < Z))
            def _():
                forward(s, d)

            return carry

        lax.fori_loop(0, E, inner, 0)
        d = k - (E - 1)

        @pl.when(d == 0)
        def _():
            pick()
            prepare()
            block(b, 0, W)

        @pl.when(d > 0)
        def _():
            both(d, unpick)
            both(d - 1, dealt)
            both(d, lambda zz: block(2 * zz + c, 0, V))

            @pl.when(d == 1)
            def _():
                def shard(s, carry):
                    own_sib(s, 1 - c).wait_recv()
                    return carry

                lax.fori_loop(0, E, shard, 0)
                block(2 * z + 1 - c, 0, W)

            both(d - 1, whole_from_sibling)
            both(d - 1, lambda zz: block(2 * zz + c, V, W))
            both(d - 2, rest_from_sibling)

        return carry

    def prepare():
        m_copy.wait()
        for k in range(1, E):
            meta_to(k).wait_send()
            other = mate(k)
            remote(meta_ref, m_ref.at[other], m_s.at[k], m_r.at[other], other, b).wait_recv()

        def row(i):
            return jnp.concatenate([m_ref[s, i:i + 1, :] for s in range(E)], axis=1)

        live = (row(0) == e) | (row(1) == e)
        count = jnp.sum(live.astype(jnp.float32), axis=1, keepdims=True)
        masked = h_ref[:, pl.ds(pl.multiple_of(b * W, 128), W)].T * live.astype(jnp.bfloat16)
        lhs[...] = masked
        classes = lax.broadcasted_iota(jnp.int32, (CLASSES, live.shape[1]), 0)
        one_hot = ((row(2) == classes) & live).astype(jnp.bfloat16)
        scale[...] = jnp.broadcast_to(1.0 / count, scale.shape)
        cross_ref[...] = lax.dot_general(
            one_hot, masked, (((1,), (1,)), ((), ())), preferred_element_type=jnp.float32) * (CLASSES / count)

    def block(blk, start, stop):
        def columns(i, carry):
            cols = pl.ds(pl.multiple_of(blk * W + i * tile, 128), tile)
            acc = jnp.dot(lhs[...], h_ref[:, cols], preferred_element_type=jnp.float32)
            moment_ref[0, :, cols] = (acc * scale[0:1, 0:1]).astype(moment_ref.dtype)
            return carry

        lax.fori_loop(start // tile, stop // tile, columns, 0)

    def whole_from_sibling(zz):
        def shard(s, carry):
            h_here(s, 2 * zz + 1 - c)
            return carry

        lax.fori_loop(0, E, shard, 0)
        block(2 * zz + 1 - c, 0, V)

    def rest_from_sibling(zz):
        def shard(s, carry):
            w_here(s, 2 * zz + 1 - c)
            return carry

        lax.fori_loop(0, E, shard, 0)
        block(2 * zz + 1 - c, V, W)

    lax.fori_loop(0, E + Z + 1, turn, 0)

    for d in range(1, Z):
        tok_z(d).wait_send()

    def finish(s, carry):
        def chips(zz, carry):
            tok_sib(s, zz).wait_send()

            @pl.when(zz == z)
            def _():
                own_sib(s, c).wait_send()

            @pl.when(zz != z)
            def _():
                h_sib(s, zz).wait_send()
                w_sib(s, zz).wait_send()

            @pl.when((zz != z) & (s > 0))
            def _():
                deal(s, zz).wait_send()

            @pl.when(s > 0)
            def _():
                tok_plane(s, zz).wait_send()

            @pl.when((zz <= z) & (z < Z - 1))
            def _():
                h_up(s, zz).wait_send()

            @pl.when((zz >= z) & (z > 0))
            def _():
                h_dn(s, zz).wait_send()

            return carry

        return lax.fori_loop(0, Z, chips, carry)

    lax.fori_loop(0, E, finish, 0)
    for k in range(1, E):
        meet(mate(k)).wait_send()

    def lines(zz, carry):
        @pl.when((zz <= z) & (z < Z - 1))
        def _():
            pq_up(zz).wait_send()

        @pl.when((zz >= z) & (z > 0))
        def _():
            pq_dn(zz).wait_send()

        return carry

    lax.fori_loop(0, Z, lines, 0)


def gather(tokens, meta, columns, gate_weight, up_weight, E, B):
    rows, F = tokens.shape
    D, W = gate_weight.shape[1:]
    Z = B // 2
    in_hbm = pl.BlockSpec(memory_space=pltpu.HBM)
    in_vmem = pl.BlockSpec(memory_space=pltpu.VMEM)
    dma = pltpu.SemaphoreType.DMA
    return pl.pallas_call(
        functools.partial(gather_kernel, E, B),
        out_shape=[pltpu.VMEM((1, W, B * W), jnp.bfloat16), jax.ShapeDtypeStruct((CLASSES, W), jnp.float32)],
        in_specs=[in_hbm, in_vmem, in_vmem, in_hbm, in_hbm],
        out_specs=[in_vmem, in_vmem],
        scratch_shapes=[
            pltpu.VMEM((E, rows, D), jnp.bfloat16),
            pltpu.VMEM((D, W), jnp.bfloat16),
            pltpu.VMEM((D, W), jnp.bfloat16),
            pltpu.VMEM((E * rows, B * W), jnp.bfloat16),
            pltpu.VMEM((E,) + meta.shape, jnp.int32),
            pltpu.VMEM((W, E * rows), jnp.bfloat16),
            pltpu.VMEM((8, 128), jnp.float32),
            dma((4,)), dma((Z,)), dma((E, Z)), dma((E, Z)), dma((E, B)), dma((E,)), dma((E,)),
            dma((E, Z)), dma((E, Z)), dma((E, Z)), dma((E, B)),
            pltpu.VMEM((2, E, rows, 128), jnp.bfloat16),
            pltpu.VMEM((E, rows, W // 2), jnp.bfloat16),
            pltpu.VMEM((Z, 2, rows, W // 2), jnp.bfloat16),
            pltpu.VMEM((Z, E, rows, W // 2), jnp.bfloat16),
            dma((E,)), dma((E,)), dma((Z,)), dma((Z,)), dma((Z,)), dma((E, Z)), dma((E, Z)), dma((E, B)),
        ],
        compiler_params=pltpu.CompilerParams(
            collective_id=0, has_side_effects=True, vmem_limit_bytes=44 * MIB),
        name="hidden_moments",
    )(tokens, meta, columns, gate_weight, up_weight)


def plain(tokens, routes, labels, gate_weight, up_weight):
    everyone = lax.all_gather(lax.all_gather(tokens, "expert", axis=0, tiled=True), "blk", axis=1, tiled=True)
    routes = lax.all_gather(routes, "expert", axis=0, tiled=True)
    labels = lax.all_gather(labels, "expert", axis=0, tiled=True)
    live = jnp.any(routes == lax.axis_index("expert"), axis=1)
    gate = jnp.dot(everyone, gate_weight[0], preferred_element_type=jnp.float32)
    up = jnp.dot(everyone, up_weight[0], preferred_element_type=jnp.float32)
    hidden = jnp.where(live[:, None], jax.nn.silu(gate) * up, 0).astype(jnp.bfloat16)
    count = jnp.sum(live.astype(jnp.float32))
    one_hot = (labels[:, None] == jnp.arange(CLASSES, dtype=jnp.int32)[None, :]).astype(jnp.bfloat16)
    over_rows = (((0,), (0,)), ((), ()))
    cross = lax.dot_general(hidden, one_hot, over_rows, preferred_element_type=jnp.float32) * (CLASSES / count)
    full = lax.all_gather(hidden, "blk", axis=1, tiled=True)
    moment = lax.dot_general(hidden, full, over_rows, preferred_element_type=jnp.float32) / count
    return moment.astype(jnp.bfloat16)[None], cross[None]


def shards(tokens, routes, labels, gate_weight, up_weight):
    E, B = lax.axis_size("expert"), lax.axis_size("blk")
    rows, F = tokens.shape
    W = gate_weight.shape[2]
    if B % 2 or F % 128 or W % 512 or rows != 128 or routes.shape[1] != 2:
        return plain(tokens, routes, labels, gate_weight, up_weight)
    meta = jnp.concatenate([routes.T, labels[None], jnp.zeros((5, rows), jnp.int32)], axis=0)
    columns = jnp.broadcast_to(routes.T[:, :, None], routes.T.shape + (128,))
    moment, cross = gather(tokens, meta, columns, gate_weight, up_weight, E, B)
    return moment, cross.T[None]


def solution(mesh):
    in_specs = (
        P("expert", "blk"),
        P("expert", None),
        P("expert"),
        P("expert", None, "blk"),
        P("expert", None, "blk"),
    )
    out_specs = (P("expert", "blk", None), P("expert", "blk", None))
    return jax.shard_map(shards, mesh=mesh, in_specs=in_specs, out_specs=out_specs, check_vma=False)
```

```python
import functools

import jax
import jax.numpy as jnp
from jax import lax
from jax.experimental import pallas as pl
from jax.experimental.pallas import tpu as pltpu
from jax.sharding import PartitionSpec as P

CLASSES = 16
MIB = 1 << 20
MESH = pl.DeviceIdType.MESH


def gather_kernel(E, B, t_ref, meta_ref, rc_ref, wg_ref, wu_ref, moment_ref, cross_ref,
                  tok, wg, wu, h_ref, m_ref, lhs, scale, loc_sem, tz_s, tsib_s, tpl_s, t_r, m_s, m_r,
                  hsib_s, hup_s, hdn_s, h_r,
                  mk, g_buf, pq, r_buf, fw_s, fw_r, pqup_s, pqdn_s, pq_r, rp_s, wsib_s, w_r):
    Z = B // 2
    rows, F = t_ref.shape
    W = wg_ref.shape[2]
    V = W // 4
    e, b = lax.axis_index("expert"), lax.axis_index("blk")
    z, c = b // 2, b % 2
    sib = b + 1 - 2 * c

    def mate(k):
        if E == 4:
            return 2 * lax.rem(e // 2 + k // 2, 2) + lax.rem(e % 2 + k % 2, 2)
        return lax.rem(e + k, E)

    g_copy = pltpu.make_async_copy(wg_ref.at[0], wg, loc_sem.at[0])
    u_copy = pltpu.make_async_copy(wu_ref.at[0], wu, loc_sem.at[1])
    g_copy.start()
    u_copy.start()

    barrier = pltpu.get_barrier_semaphore()

    def to(expert, blk):
        return {"expert": expert, "blk": blk}

    def greet(expert, blk):
        pl.semaphore_signal(barrier, inc=1, device_id=to(expert, blk), device_id_type=MESH)

    greet(e, sib)
    for d in range(1, Z):
        greet(e, 2 * lax.rem(z + d, Z) + c)
    for k in range(1, E):
        greet(mate(k), b)
    pl.semaphore_wait(barrier, Z + E - 1)

    def chunk(s, blk):
        return tok.at[s, :, pl.ds(pl.multiple_of(blk * F, 128), F)]

    def part(s, blk, start, width):
        return h_ref.at[pl.ds(pl.multiple_of(s * rows, rows), rows),
                        pl.ds(pl.multiple_of(blk * W + start, 128), width)]

    def piece(s, blk):
        return part(s, blk, 0, V)

    def rest(s, blk):
        return part(s, blk, V, W - V)

    def remote(src, dst, send, recv, expert, blk):
        return pltpu.make_async_remote_copy(
            src_ref=src, dst_ref=dst, send_sem=send, recv_sem=recv,
            device_id=to(expert, blk), device_id_type=MESH)

    def tok_z(d):
        return remote(t_ref, chunk(e, b), tz_s.at[d], t_r.at[e, b], e, 2 * lax.rem(z + d, Z) + c)

    def tok_sib(s, zz, src=None):
        blk = 2 * zz + c
        return remote(chunk(s, blk) if src is None else src, chunk(s, blk), tsib_s.at[s, zz], t_r.at[s, blk], e, sib)

    def tok_plane(k, zz, src=None):
        blk = 2 * zz + c
        return remote(chunk(e, blk) if src is None else src, chunk(e, blk), tpl_s.at[k, zz], t_r.at[e, blk],
                      mate(k), b)

    def tok_here(s, blk):
        remote(chunk(s, blk), chunk(s, blk), tz_s.at[0], t_r.at[s, blk], e, sib).wait_recv()

    def meta_to(k):
        return remote(meta_ref, m_ref.at[e], m_s.at[k], m_r.at[e], mate(k), b)

    t_copy = pltpu.make_async_copy(t_ref, chunk(e, b), loc_sem.at[2])
    m_copy = pltpu.make_async_copy(meta_ref, m_ref.at[e], loc_sem.at[3])
    for d in range(1, Z):
        tok_z(d).start()
    tok_sib(e, z, t_ref).start()
    for k in range(1, E - 1):
        tok_plane(k, z, t_ref).start()
    t_copy.start()
    m_copy.start()
    for k in range(1, E):
        meta_to(k).start()

    def h_sib(s, zz):
        blk = 2 * zz + c
        return remote(piece(s, blk), piece(s, blk), hsib_s.at[s, zz], h_r.at[s, blk], e, sib)

    def own_sib(s, core):
        blk = 2 * z + core
        return remote(part(s, blk, 0, W), part(s, blk, 0, W), hsib_s.at[s, z], h_r.at[s, blk], e, sib)

    def meet(s):
        return remote(rest(s, b), g_buf.at[e], fw_s.at[s], fw_r.at[e], s, b)

    def pq_up(zz):
        return remote(pq.at[zz], pq.at[zz], pqup_s.at[zz], pq_r.at[zz], e, b + 2)

    def pq_dn(zz):
        return remote(pq.at[zz], pq.at[zz], pqdn_s.at[zz], pq_r.at[zz], e, b - 2)

    def deal(k, zz):
        blk = 2 * zz + c
        return remote(r_buf.at[zz, k], rest(e, blk), rp_s.at[k, zz], w_r.at[e, blk], mate(k), b)

    def w_sib(s, zz):
        blk = 2 * zz + c
        return remote(rest(s, blk), rest(s, blk), wsib_s.at[s, zz], w_r.at[s, blk], e, sib)

    def w_here(s, blk):
        remote(rest(s, blk), rest(s, blk), wsib_s.at[s, 0], w_r.at[s, blk], e, sib).wait_recv()

    def pass_on(zz):
        @pl.when((zz <= z) & (z < Z - 1))
        def _():
            pq_up(zz).start()

        @pl.when((zz >= z) & (z > 0))
        def _():
            pq_dn(zz).start()

    def pick():
        for k in range(1, E):
            other = mate(k)
            remote(rest(e, b), g_buf.at[other], fw_s.at[other], fw_r.at[other], other, b).wait_recv()

        def lanes(i, carry):
            cols = pl.ds(pl.multiple_of(i * 128, 128), 128)
            mine = h_ref[pl.ds(pl.multiple_of(e * rows, rows), rows),
                         pl.ds(pl.multiple_of(b * W + V + i * 128, 128), 128)]
            for top in range(2):
                total = mine * mk[top, e]
                for k in range(1, E):
                    other = mate(k)
                    total += g_buf[other, :, cols] * mk[top, other]
                pq[z, top, :, cols] = total
            return carry

        lax.fori_loop(0, (W - V) // 128, lanes, 0)
        pass_on(z)

    def unpick(zz):
        remote(pq.at[zz], pq.at[zz], pqup_s.at[zz], pq_r.at[zz], e, sib).wait_recv()
        pass_on(zz)
        blk = 2 * zz + c

        def lanes(i, carry):
            cols = pl.ds(pl.multiple_of(i * 128, 128), 128)
            first, second = pq[zz, 0, :, cols], pq[zz, 1, :, cols]
            for k in range(E):
                other = mate(k)
                value = first * mk[0, other] + second * mk[1, other]
                if k:
                    r_buf[zz, k, :, cols] = value
                else:
                    h_ref[pl.ds(pl.multiple_of(e * rows, rows), rows),
                          pl.ds(pl.multiple_of(blk * W + V + i * 128, 128), 128)] = value
            return carry

        lax.fori_loop(0, (W - V) // 128, lanes, 0)
        for k in range(1, E):
            deal(k, zz).start()
        w_sib(e, zz).start()

    def dealt(zz):
        for k in range(1, E):
            s = mate(k)
            w_here(s, 2 * zz + c)
            w_sib(s, zz).start()

    def both(d, action):
        @pl.when((d > 0) & (d < Z) & (z - d >= 0))
        def _():
            action(z - d)

        @pl.when((d > 0) & (z + d < Z))
        def _():
            action(z + d)

    for top in range(2):
        for k in range(E):
            mk[top, k] = (rc_ref[top] == k).astype(mk.dtype)

    def h_up(s, zz):
        blk = 2 * zz + c
        return remote(piece(s, blk), piece(s, blk), hup_s.at[s, zz], h_r.at[s, blk], e, b + 2)

    def h_dn(s, zz):
        blk = 2 * zz + c
        return remote(piece(s, blk), piece(s, blk), hdn_s.at[s, zz], h_r.at[s, blk], e, b - 2)

    def h_here(s, blk):
        remote(piece(s, blk), piece(s, blk), hsib_s.at[s, 0], h_r.at[s, blk], e, sib).wait_recv()

    tile = min(W, 256)

    def compute(j, s):
        @pl.when(j == 0)
        def _():
            def arrived(d, carry):
                zz = lax.rem(z + d, Z)
                tok_here(e, 2 * zz + c)
                tok_sib(e, zz).start()
                for k in range(1, E - 1):
                    tok_plane(k, zz).start()
                return carry

            lax.fori_loop(1, Z, arrived, 0)
            t_copy.wait()

            def across(zz, carry):
                tok_plane(E - 1, zz).start()
                return carry

            lax.fori_loop(0, Z, across, 0)
            g_copy.wait()
            u_copy.wait()

        @pl.when(j > 0)
        def _():
            def arrived(d, carry):
                zz = lax.rem(z + d, Z)
                tok_here(s, 2 * zz + c)
                tok_sib(s, zz).start()
                return carry

            lax.fori_loop(0, Z, arrived, 0)

        def other(zz, carry):
            tok_here(s, 2 * zz + 1 - c)
            return carry

        lax.fori_loop(0, Z, other, 0)

        def columns(i, carry):
            cols = pl.ds(pl.multiple_of(i * tile, tile), tile)
            x = tok[s]
            gate = jnp.dot(x, wg[:, cols], preferred_element_type=jnp.float32)
            up = jnp.dot(x, wu[:, cols], preferred_element_type=jnp.float32)
            h_ref[pl.ds(pl.multiple_of(s * rows, rows), rows),
                  pl.ds(pl.multiple_of(b * W + i * tile, 128), tile)] = (
                gate / (1.0 + jnp.exp(-gate)) * up).astype(h_ref.dtype)
            return carry

        lax.fori_loop(0, W // tile, columns, 0)

        @pl.when(z < Z - 1)
        def _():
            h_up(s, z).start()

        @pl.when(z > 0)
        def _():
            h_dn(s, z).start()

        own_sib(s, c).start()

        @pl.when(j > 0)
        def _():
            meet(s).start()

    def forward(s, d):
        @pl.when(z - d >= 0)
        def _():
            h_here(s, 2 * (z - d) + c)

            @pl.when(z < Z - 1)
            def _():
                h_up(s, z - d).start()

            h_sib(s, z - d).start()

        @pl.when(z + d < Z)
        def _():
            h_here(s, 2 * (z + d) + c)

            @pl.when(z > 0)
            def _():
                h_dn(s, z + d).start()

            h_sib(s, z + d).start()

    def turn(k, carry):
        def inner(i, carry):
            j = E - 1 - i
            s = mate(j)
            d = k - j

            @pl.when(d == 0)
            def _():
                compute(j, s)

            @pl.when((d > 0) & (d < Z))
            def _():
                forward(s, d)

            return carry

        lax.fori_loop(0, E, inner, 0)
        d = k - (E - 1)

        @pl.when(d == 0)
        def _():
            pick()
            prepare()
            block(b, 0, W)

        @pl.when(d > 0)
        def _():
            both(d, unpick)
            both(d - 1, dealt)
            both(d, lambda zz: block(2 * zz + c, 0, V))

            @pl.when(d == 1)
            def _():
                def shard(s, carry):
                    own_sib(s, 1 - c).wait_recv()
                    return carry

                lax.fori_loop(0, E, shard, 0)
                block(2 * z + 1 - c, 0, W)

            both(d - 1, whole_from_sibling)
            both(d - 1, lambda zz: block(2 * zz + c, V, W))
            both(d - 2, rest_from_sibling)

        return carry

    def prepare():
        m_copy.wait()
        for k in range(1, E):
            meta_to(k).wait_send()
            other = mate(k)
            remote(meta_ref, m_ref.at[other], m_s.at[k], m_r.at[other], other, b).wait_recv()

        def row(i):
            return jnp.concatenate([m_ref[s, i:i + 1, :] for s in range(E)], axis=1)

        live = (row(0) == e) | (row(1) == e)
        count = jnp.sum(live.astype(jnp.float32), axis=1, keepdims=True)
        masked = h_ref[:, pl.ds(pl.multiple_of(b * W, 128), W)].T * live.astype(jnp.bfloat16)
        lhs[...] = masked
        classes = lax.broadcasted_iota(jnp.int32, (CLASSES, live.shape[1]), 0)
        one_hot = ((row(2) == classes) & live).astype(jnp.bfloat16)
        scale[...] = jnp.broadcast_to(1.0 / count, scale.shape)
        cross_ref[...] = lax.dot_general(
            one_hot, masked, (((1,), (1,)), ((), ())), preferred_element_type=jnp.float32) * (CLASSES / count)

    def block(blk, start, stop):
        def columns(i, carry):
            cols = pl.ds(pl.multiple_of(blk * W + i * tile, 128), tile)
            acc = jnp.dot(lhs[...], h_ref[:, cols], preferred_element_type=jnp.float32)
            moment_ref[0, :, cols] = (acc * scale[0:1, 0:1]).astype(moment_ref.dtype)
            return carry

        lax.fori_loop(start // tile, stop // tile, columns, 0)

    def whole_from_sibling(zz):
        def shard(s, carry):
            h_here(s, 2 * zz + 1 - c)
            return carry

        lax.fori_loop(0, E, shard, 0)
        block(2 * zz + 1 - c, 0, V)

    def rest_from_sibling(zz):
        def shard(s, carry):
            w_here(s, 2 * zz + 1 - c)
            return carry

        lax.fori_loop(0, E, shard, 0)
        block(2 * zz + 1 - c, V, W)

    lax.fori_loop(0, E + Z + 1, turn, 0)

    for d in range(1, Z):
        tok_z(d).wait_send()

    def finish(s, carry):
        def chips(zz, carry):
            tok_sib(s, zz).wait_send()

            @pl.when(zz == z)
            def _():
                own_sib(s, c).wait_send()

            @pl.when(zz != z)
            def _():
                h_sib(s, zz).wait_send()
                w_sib(s, zz).wait_send()

            @pl.when((zz != z) & (s > 0))
            def _():
                deal(s, zz).wait_send()

            @pl.when(s > 0)
            def _():
                tok_plane(s, zz).wait_send()

            @pl.when((zz <= z) & (z < Z - 1))
            def _():
                h_up(s, zz).wait_send()

            @pl.when((zz >= z) & (z > 0))
            def _():
                h_dn(s, zz).wait_send()

            return carry

        return lax.fori_loop(0, Z, chips, carry)

    lax.fori_loop(0, E, finish, 0)
    for k in range(1, E):
        meet(mate(k)).wait_send()

    def lines(zz, carry):
        @pl.when((zz <= z) & (z < Z - 1))
        def _():
            pq_up(zz).wait_send()

        @pl.when((zz >= z) & (z > 0))
        def _():
            pq_dn(zz).wait_send()

        return carry

    lax.fori_loop(0, Z, lines, 0)


def gather(tokens, meta, columns, gate_weight, up_weight, E, B):
    rows, F = tokens.shape
    D, W = gate_weight.shape[1:]
    Z = B // 2
    in_hbm = pl.BlockSpec(memory_space=pltpu.HBM)
    in_vmem = pl.BlockSpec(memory_space=pltpu.VMEM)
    dma = pltpu.SemaphoreType.DMA
    return pl.pallas_call(
        functools.partial(gather_kernel, E, B),
        out_shape=[pltpu.VMEM((1, W, B * W), jnp.bfloat16), jax.ShapeDtypeStruct((CLASSES, W), jnp.float32)],
        in_specs=[in_hbm, in_vmem, in_vmem, in_hbm, in_hbm],
        out_specs=[in_vmem, in_vmem],
        scratch_shapes=[
            pltpu.VMEM((E, rows, D), jnp.bfloat16),
            pltpu.VMEM((D, W), jnp.bfloat16),
            pltpu.VMEM((D, W), jnp.bfloat16),
            pltpu.VMEM((E * rows, B * W), jnp.bfloat16),
            pltpu.VMEM((E,) + meta.shape, jnp.int32),
            pltpu.VMEM((W, E * rows), jnp.bfloat16),
            pltpu.VMEM((8, 128), jnp.float32),
            dma((4,)), dma((Z,)), dma((E, Z)), dma((E, Z)), dma((E, B)), dma((E,)), dma((E,)),
            dma((E, Z)), dma((E, Z)), dma((E, Z)), dma((E, B)),
            pltpu.VMEM((2, E, rows, 128), jnp.bfloat16),
            pltpu.VMEM((E, rows, W - W // 4), jnp.bfloat16),
            pltpu.VMEM((Z, 2, rows, W - W // 4), jnp.bfloat16),
            pltpu.VMEM((Z, E, rows, W - W // 4), jnp.bfloat16),
            dma((E,)), dma((E,)), dma((Z,)), dma((Z,)), dma((Z,)), dma((E, Z)), dma((E, Z)), dma((E, B)),
        ],
        compiler_params=pltpu.CompilerParams(
            collective_id=0, has_side_effects=True, vmem_limit_bytes=44 * MIB),
        name="hidden_moments",
    )(tokens, meta, columns, gate_weight, up_weight)


def plain(tokens, routes, labels, gate_weight, up_weight):
    everyone = lax.all_gather(lax.all_gather(tokens, "expert", axis=0, tiled=True), "blk", axis=1, tiled=True)
    routes = lax.all_gather(routes, "expert", axis=0, tiled=True)
    labels = lax.all_gather(labels, "expert", axis=0, tiled=True)
    live = jnp.any(routes == lax.axis_index("expert"), axis=1)
    gate = jnp.dot(everyone, gate_weight[0], preferred_element_type=jnp.float32)
    up = jnp.dot(everyone, up_weight[0], preferred_element_type=jnp.float32)
    hidden = jnp.where(live[:, None], jax.nn.silu(gate) * up, 0).astype(jnp.bfloat16)
    count = jnp.sum(live.astype(jnp.float32))
    one_hot = (labels[:, None] == jnp.arange(CLASSES, dtype=jnp.int32)[None, :]).astype(jnp.bfloat16)
    over_rows = (((0,), (0,)), ((), ()))
    cross = lax.dot_general(hidden, one_hot, over_rows, preferred_element_type=jnp.float32) * (CLASSES / count)
    full = lax.all_gather(hidden, "blk", axis=1, tiled=True)
    moment = lax.dot_general(hidden, full, over_rows, preferred_element_type=jnp.float32) / count
    return moment.astype(jnp.bfloat16)[None], cross[None]


def shards(tokens, routes, labels, gate_weight, up_weight):
    E, B = lax.axis_size("expert"), lax.axis_size("blk")
    rows, F = tokens.shape
    W = gate_weight.shape[2]
    if B % 2 or F % 128 or W % 1024 or rows != 128 or routes.shape[1] != 2:
        return plain(tokens, routes, labels, gate_weight, up_weight)
    meta = jnp.concatenate([routes.T, labels[None], jnp.zeros((5, rows), jnp.int32)], axis=0)
    columns = jnp.broadcast_to(routes.T[:, :, None], routes.T.shape + (128,))
    moment, cross = gather(tokens, meta, columns, gate_weight, up_weight, E, B)
    return moment, cross.T[None]


def solution(mesh):
    in_specs = (
        P("expert", "blk"),
        P("expert", None),
        P("expert"),
        P("expert", None, "blk"),
        P("expert", None, "blk"),
    )
    out_specs = (P("expert", "blk", None), P("expert", "blk", None))
    return jax.shard_map(shards, mesh=mesh, in_specs=in_specs, out_specs=out_specs, check_vma=False)
```
